32 devices in a mesh: gz: 16 (over z, x, core), xy: 2 (over y).
Axes of the slice: x: 2, y: 2, z: 4, core: 2. Of those that a mesh axis runs over, the one named last changes fastest.
Arguments:
- moments: bfloat16 [361, 128, 256], P(None, 'gz', 'xy'), may hold values from -4 to 4
- counts: int32 [128, 256], P('gz', 'xy'), may hold values from 0 to 7
- m2x: bfloat16 [1296, 361], replicated, may hold values from -0.3125 to 0.3125
- x2l: bfloat16 [361, 1296], replicated, may hold values from -0.0625 to 0.0625
- decay_rate: float32 [648], replicated, may hold values from 0.001953125 to 0.05
- wave_x: float32 [648], replicated, may hold values from -3.140625 to 3.140625
- wave_y: float32 [648], replicated, may hold values from -3.140625 to 3.140625
- offsets: int32 [6, 2], replicated, may hold values from -2 to 2, as said below
Outputs:
- local_out: bfloat16 [361, 128, 256], P(None, 'gz', 'xy')
The draws below stay inside these ranges and needn't reach their ends.
Inputs may be any that keep to these rules, and one draw needn't show every extreme that they name: `offsets`: some row is (2, -2) and some row is (-2, 2).
All inputs are finite; a program needn't handle non-finite values.
Results may differ from the reference program's by a relative error of at most 0.0064.
Values may be sent and summed in bfloat16 or wider, within the bound.
A program may use at most 192 MiB of HBM per device.

```python
import math
import jax
import jax.numpy as jnp
from jax import lax

MC = 361
NE = 648
BY = 8
R = 2
NOFF = 6
NZ = 128
NX = 32
NXY = 256


def draw_offsets(key, part):
    values = jax.random.randint(key, (NOFF, 2), -R, R + 1).astype(jnp.int32)
    values = values.at[0].set(jnp.array([R, -R], jnp.int32))
    values = values.at[1].set(jnp.array([-R, R], jnp.int32))
    return values


def set_ends(drawn, key, low, largest):
    place = [jax.random.randint(jax.random.fold_in(key, axis), (), 0, length) for axis, length in enumerate(drawn.shape)]
    longest = drawn.shape.index(max(drawn.shape))
    next_to = place[:longest] + [(place[longest] + 1) % drawn.shape[longest]] + place[longest + 1:]
    return drawn.at[tuple(place)].set(low).at[tuple(next_to)].set(largest)


def block_scale(rng, shape, shards, smallest, top_value):
    factor_of, own = 1.0, jax.random.fold_in(rng, 6)
    for position, shards_of in shards:
        steps = jnp.exp(jax.random.uniform(jax.random.fold_in(own, position), (shards_of,), jnp.float32, smallest / len(shards), top_value / len(shards)))
        factor_of = factor_of * jnp.repeat(steps, shape[position] // shards_of).reshape([-1 if axis == position else 1 for axis in range(len(shape))])
    return factor_of


def noise(own_key, shape, width, limit, split=(), kind=jnp.bfloat16):
    gain = block_scale(own_key, shape, split, -0.22, 0.18) if split else 1.0
    values = jax.random.normal(own_key, shape, jnp.float32) * width * gain
    return jnp.minimum(jnp.maximum(values, -limit), limit).astype(kind)


def setup_inputs(seed: int = 0) -> dict:
    key_list = jax.random.split(jax.random.key(seed), 9)
    return {
        "moments": noise(key_list[0], (MC, NZ, NXY), 0.3, 4.0, ((1, 16), (2, 2))),
        "counts": set_ends(jax.random.randint(key_list[1], (NZ, NXY), 0, 8), jax.random.fold_in(key_list[1], 1), 0, 7).astype(jnp.int32),
        "m2x": noise(key_list[2], (2 * NE, MC), MC ** -0.5, 0.3125),
        "x2l": noise(key_list[3], (MC, 2 * NE), (2 * NE * NOFF) ** -0.5, 0.0625),
        "decay_rate": jnp.clip(jnp.exp(jax.random.uniform(key_list[4], (NE,), jnp.float32, math.log(0.001953125), math.log(0.05))), 0.001953125, 0.05),
        "wave_x": jnp.clip(jax.random.uniform(key_list[5], (NE,), jnp.float32, -3.140625, 3.140625), -3.140625, 3.140625),
        "wave_y": jnp.clip(jax.random.uniform(key_list[6], (NE,), jnp.float32, -3.140625, 3.140625), -3.140625, 3.140625),
        "offsets": draw_offsets(jax.random.fold_in(key_list[8], 71), 0),
    }


def reference(moments, counts, m2x, x2l, decay_rate, wave_x, wave_y, offsets):
    exp_rows = 2 * NE
    rate_col = jnp.concatenate([decay_rate, decay_rate])[:, None]
    factor = jnp.exp(-rate_col)
    weight = jnp.sqrt(1.0 - factor * factor)

    def layer_terms(layer):
        coeff_layer = lax.dynamic_index_in_dim(moments, layer, 1, keepdims=False).astype(jnp.float32)
        count_layer = lax.dynamic_index_in_dim(counts, layer, 0, keepdims=False).astype(jnp.float32)
        multipole = (coeff_layer * count_layer[None, :]).astype(jnp.bfloat16)
        return weight * jnp.dot(m2x, multipole, preferred_element_type=jnp.float32)

    def local_from(upward):
        field_grid = upward.reshape(exp_rows, NX, BY)
        acc_real = jnp.zeros((NE, NX, BY), jnp.float32)
        acc_imag = jnp.zeros((NE, NX, BY), jnp.float32)
        for list_entry in range(NOFF):
            step_x = offsets[list_entry, 0]
            step_y = offsets[list_entry, 1]
            moved = jnp.roll(field_grid, (step_x, step_y), axis=(1, 2))
            phase_angle = wave_x * step_x.astype(jnp.float32) + wave_y * step_y.astype(jnp.float32)
            cosine = jnp.cos(phase_angle)[:, None, None]
            sine_part = jnp.sin(phase_angle)[:, None, None]
            part_real = moved[:NE].astype(jnp.float32)
            part_imag = moved[NE:].astype(jnp.float32)
            acc_real = acc_real + part_real * cosine - part_imag * sine_part
            acc_imag = acc_imag + part_real * sine_part + part_imag * cosine
        shifted = jnp.concatenate([acc_real, acc_imag], axis=0).astype(jnp.bfloat16).reshape(exp_rows, NXY)
        return jnp.dot(x2l, shifted, preferred_element_type=jnp.float32).astype(jnp.bfloat16)

    def first_pass(carry, layer):
        state, prev_term = carry
        fresh = layer_terms(layer)
        return ((factor * state + fresh, fresh), None)
    zero_state = jnp.zeros((exp_rows, NXY), jnp.float32)
    layer_ids = jnp.arange(NZ, dtype=jnp.int32)
    (lap_state, last_term), _ = lax.scan(first_pass, (zero_state, zero_state), layer_ids)
    lap_gain = 1.0 - jnp.exp(-rate_col * NZ)

    def second_pass(carry, layer):
        state, prev_term = carry
        upward = (factor * (state - prev_term)).astype(jnp.bfloat16)
        local_layer = local_from(upward)
        fresh = layer_terms(layer)
        return ((factor * state + fresh, fresh), local_layer)
    _, layer_out = lax.scan(second_pass, (lap_state / lap_gain, last_term), layer_ids)
    return jnp.transpose(layer_out, (1, 0, 2))
```

```python
import functools

import jax
import jax.numpy as jnp
from jax import lax
from jax.experimental import pallas as pl
from jax.experimental.pallas import tpu as pltpu
from jax.sharding import PartitionSpec as P

BY = 8
R = 2
NOFF = 6
GROUP = 4
BOXES = 128
MESH = pl.DeviceIdType.MESH
F32 = jnp.float32
BF16 = jnp.bfloat16


def up(value, step):
    return -(-value // step) * step


def kernel(
    loop_size, layers, rows,
    off_ref, mp_ref, m2x_ref, xs_ref, cs_ref, rate_ref,
    out_ref,
    terms, outgo, top, below, ingroup, planes, entbuf, enter, wall, upward, perm, place, mixed,
    own, edge, edge_out, edge_in,
    top_s, top_r, a_s, a_r, b_s, b_r, c_s, c_r, e_s, e_r,
):
    slab = lax.axis_index("gz")
    half = lax.axis_index("xy")
    groups = loop_size // GROUP
    group, member = slab // GROUP, lax.rem(slab, GROUP)
    after = lax.rem(slab + 1, loop_size)
    before = lax.rem(slab + loop_size - 1, loop_size)
    padded = outgo.shape[0]
    quarter = padded // GROUP
    out_rows = out_ref.shape[0]
    coeffs = m2x_ref.shape[1]

    def mate(step):
        return lax.rem(member + step, GROUP)

    def mate_id(step):
        return group * GROUP + mate(step)

    def plane_id(step):
        return lax.rem(group + step, groups) * GROUP + member

    barrier = pltpu.get_barrier_semaphore()
    partners = [after, before]
    partners += [mate_id(step) for step in range(1, GROUP)]
    partners += [plane_id(step) for step in range(1, groups)]
    for partner in partners:
        pl.semaphore_signal(barrier, inc=1, device_id={"gz": partner}, device_id_type=MESH)
    pl.semaphore_signal(barrier, inc=1, device_id={"xy": 1 - half}, device_id_type=MESH)
    pl.semaphore_wait(barrier, len(partners) + 1)

    top_copy = pltpu.make_async_remote_copy(
        src_ref=mp_ref.at[:, pl.ds((layers - 1) * BOXES, BOXES)],
        dst_ref=top, send_sem=top_s, recv_sem=top_r,
        device_id={"gz": after}, device_id_type=MESH,
    )
    top_copy.start()

    block = rows // 3

    @pl.loop(0, 3)
    def _(turn):
        at = pl.ds(pl.multiple_of(turn * block, 16), block)
        terms[at, :] = jnp.dot(m2x_ref[at, :], mp_ref[0:coeffs, :], preferred_element_type=F32)

    @pl.loop(0, rows // 16)
    def _(turn):
        at = pl.ds(pl.multiple_of(turn * 16, 16), 16)
        factor = jnp.exp(-rate_ref[at, :])
        square = factor * factor
        weight = jnp.sqrt(1.0 - square)
        box = [weight * terms[at, z * BOXES:(z + 1) * BOXES] for z in range(layers)]
        total = box[0]
        for z in range(1, layers):
            total = factor * total + box[z]
        outgo[at, :] = total.astype(BF16)
        state = jnp.zeros_like(factor)
        for z in range(2, layers):
            state = factor * state + square * box[z - 2]
            terms[at, z * BOXES:(z + 1) * BOXES] = state

    outgo[rows:padded, :] = jnp.zeros((padded - rows, BOXES), BF16)

    a_copies = []
    for step in range(1, GROUP):
        copy = pltpu.make_async_remote_copy(
            src_ref=outgo.at[pl.ds(pl.multiple_of(mate(step) * quarter, 16), quarter), :],
            dst_ref=ingroup.at[step], send_sem=a_s.at[step], recv_sem=a_r.at[step],
            device_id={"gz": mate_id(step)}, device_id_type=MESH,
        )
        copy.start()
        a_copies.append(copy)
    mine = pl.ds(pl.multiple_of(member * quarter, 16), quarter)
    ingroup[0] = outgo[mine, :]

    @pl.loop(0, out_rows // 16)
    def _(turn):
        real = xs_ref[pl.ds(pl.multiple_of(turn * 16, 16), 16), :].astype(F32)
        swap = xs_ref[pl.ds(pl.multiple_of(out_rows + turn * 16, 16), 16), :].astype(F32)
        for entry in range(NOFF):
            mix = real * cs_ref[entry:entry + 1, :] + swap * cs_ref[8 + entry:9 + entry, :]
            wall[pl.ds(pl.multiple_of(entry * out_rows + turn * 16, 16), 16), :] = mix.astype(BF16)

    lane = lax.broadcasted_iota(jnp.int32, (BOXES, 2 * BOXES), 0)
    column = lax.broadcasted_iota(jnp.int32, (BOXES, 2 * BOXES), 1)
    width = BOXES // BY
    for entry in range(NOFF):
        moved_x = lane // BY + off_ref[entry, 0]
        moved_y = (lane + off_ref[entry, 1]) & (BY - 1)
        inside = moved_x * BY + moved_y
        low = (moved_x + R) * BY + moved_y + BOXES
        high = (moved_x - width + R) * BY + moved_y + BOXES
        stays = (moved_x >= 0) & (moved_x < width)
        outside = jnp.where(moved_x < 0, low, high)
        for slot in range(4):
            target = jnp.where(stays, inside, outside + slot * 2 * R * BY)
            perm[slot, entry * BOXES:(entry + 1) * BOXES, :] = jnp.where(
                column == target, 1.0, 0.0).astype(BF16)
    lane = lax.broadcasted_iota(jnp.int32, (BOXES, BOXES), 0)
    column = lax.broadcasted_iota(jnp.int32, (BOXES, BOXES), 1)
    for slot in range(4):
        inner = lane - slot * 2 * R * BY
        target = jnp.where(inner < R * BY, inner + BOXES - R * BY, inner - R * BY)
        hit = (inner >= 0) & (inner < 2 * R * BY) & (column == target)
        place[slot] = jnp.where(hit, 1.0, 0.0).astype(BF16)

    for copy in a_copies:
        copy.wait_recv()

    def source(index):
        return ingroup[lax.rem(member - index + GROUP, GROUP)].astype(F32)

    rate = rate_ref[mine, :]
    decay = jnp.exp(-rate * layers)
    total = source(0)
    for index in range(1, GROUP):
        total = decay * total + source(index)
    planes[0] = total.astype(BF16)
    b_copies = []
    for step in range(1, groups):
        copy = pltpu.make_async_remote_copy(
            src_ref=planes.at[0],
            dst_ref=planes.at[step], send_sem=b_s.at[step], recv_sem=b_r.at[step],
            device_id={"gz": plane_id(step)}, device_id_type=MESH,
        )
        copy.start()
        b_copies.append(copy)

    top_copy.wait_recv()

    @pl.loop(0, 3)
    def _(turn):
        at = pl.ds(pl.multiple_of(turn * block, 16), block)
        below[at, :] = jnp.dot(m2x_ref[at, :], top[0:coeffs, :], preferred_element_type=F32)

    for copy in b_copies:
        copy.wait_recv()
    plane_decay = jnp.exp(-rate * (layers * GROUP))
    total = planes[0].astype(F32)
    for step in range(groups - 1, 0, -1):
        total = plane_decay * total + planes[step].astype(F32)
    state = total / (1.0 - jnp.exp(-rate * (layers * loop_size)))
    entbuf[0] = state.astype(BF16)
    for index in range(1, GROUP):
        state = decay * state + source(index - 1)
        entbuf[index] = state.astype(BF16)

    c_copies = []
    for step in range(1, GROUP):
        copy = pltpu.make_async_remote_copy(
            src_ref=entbuf.at[mate(step)],
            dst_ref=enter.at[mine, :],
            send_sem=c_s.at[step], recv_sem=c_r.at[step],
            device_id={"gz": mate_id(step)}, device_id_type=MESH,
        )
        copy.start()
        c_copies.append(copy)
    enter[mine, :] = entbuf[member]
    for step in range(1, GROUP):
        sender = lax.rem(member - step + GROUP, GROUP)
        pltpu.make_async_remote_copy(
            src_ref=entbuf.at[0],
            dst_ref=enter.at[pl.ds(pl.multiple_of(sender * quarter, 16), quarter), :],
            send_sem=c_s.at[step], recv_sem=c_r.at[step],
            device_id={"gz": mate_id(step)}, device_id_type=MESH,
        ).wait_recv()

    @pl.loop(0, rows // 16)
    def _(turn):
        at = pl.ds(pl.multiple_of(turn * 16, 16), 16)
        factor = jnp.exp(-rate_ref[at, :])
        weight = jnp.sqrt(1.0 - factor * factor)
        state = factor * enter[at, :].astype(F32)
        upward[at, 0:BOXES] = (state - factor * (weight * below[at, :])).astype(BF16)
        state = factor * state
        upward[at, BOXES:2 * BOXES] = state.astype(BF16)
        for z in range(2, layers):
            state = factor * state
            upward[at, z * BOXES:(z + 1) * BOXES] = (
                state + terms[at, z * BOXES:(z + 1) * BOXES]).astype(BF16)

    e_copies = []
    for pair in range(layers // 2):
        @pl.loop(0, NOFF)
        def _(entry):
            part = jnp.dot(
                wall[pl.ds(pl.multiple_of(entry * out_rows, 16), out_rows), :],
                upward[:, pair * 2 * BOXES:(pair + 1) * 2 * BOXES],
                preferred_element_type=F32,
            ).astype(BF16)
            at = pl.ds(pl.multiple_of(entry * BOXES, BOXES), BOXES)
            mixed[0, :, at] = part[:, :BOXES]
            mixed[1, :, at] = part[:, BOXES:]

        for inner in range(2):
            z = pair * 2 + inner
            placed = jnp.dot(mixed[inner], perm[z % 4], preferred_element_type=F32)
            own[:, z * BOXES:(z + 1) * BOXES] = placed[:, :BOXES]
            if z % 4 == 0:
                edge[...] = placed[:, BOXES:]
            else:
                edge[...] += placed[:, BOXES:]
        if pair % 2 == 1:
            side = pair // 2
            edge_out[side] = edge[...].astype(BF16)
            copy = pltpu.make_async_remote_copy(
                src_ref=edge_out.at[side], dst_ref=edge_in.at[side],
                send_sem=e_s.at[side], recv_sem=e_r.at[side],
                device_id={"xy": 1 - half}, device_id_type=MESH,
            )
            copy.start()
            e_copies.append(copy)

    for side, copy in enumerate(e_copies):
        copy.wait_recv()
        for slot in range(4):
            at = slice((side * 4 + slot) * BOXES, (side * 4 + slot + 1) * BOXES)
            out_ref[:, at] = (
                own[:, at] + jnp.dot(edge_in[side], place[slot], preferred_element_type=F32)
            ).astype(BF16)

    for copy in [top_copy] + a_copies + b_copies + c_copies + e_copies:
        copy.wait_send()


def body(moments, counts, m2x, x2l, decay_rate, wave_x, wave_y, offsets):
    coeffs, layers, plane_size = moments.shape
    rows = m2x.shape[0]
    loop_size = lax.axis_size("gz")
    groups = loop_size // GROUP
    padded = up(rows, 16 * GROUP)
    quarter = padded // GROUP
    in_rows = up(coeffs, 16)
    lanes = layers * plane_size

    multipole = (moments.astype(F32) * counts.astype(F32)[None]).astype(BF16)
    multipole = jnp.pad(multipole.reshape(coeffs, lanes), ((0, in_rows - coeffs), (0, 0)))
    swapped = jnp.concatenate([x2l[:, rows // 2:], x2l[:, :rows // 2]], axis=1)
    spare = ((0, in_rows - coeffs), (0, 0))
    maps = jnp.concatenate([jnp.pad(x2l, spare), jnp.pad(swapped, spare)], axis=0)
    steps = offsets.astype(F32)
    angle = steps[:, :1] * wave_x[None] + steps[:, 1:] * wave_y[None]
    cosine, sine = jnp.cos(angle), jnp.sin(angle)
    gap = jnp.zeros((2, rows), F32)
    phases = jnp.concatenate([
        jnp.concatenate([cosine, cosine], axis=1), gap,
        jnp.concatenate([sine, -sine], axis=1), gap], axis=0)
    rate = jnp.concatenate([decay_rate, decay_rate, jnp.full((padded - rows,), 0.01, F32)])
    rate = jnp.broadcast_to(rate[:, None], (padded, BOXES))

    vmem = pl.BlockSpec(memory_space=pltpu.VMEM)
    dma = pltpu.SemaphoreType.DMA
    out = pl.pallas_call(
        functools.partial(kernel, loop_size, layers, rows),
        out_shape=jax.ShapeDtypeStruct((in_rows, lanes), BF16),
        in_specs=[pl.BlockSpec(memory_space=pltpu.SMEM)] + [vmem] * 5,
        out_specs=vmem,
        scratch_shapes=[
            pltpu.VMEM((rows, lanes), F32),
            pltpu.VMEM((padded, BOXES), BF16),
            pltpu.VMEM((in_rows, BOXES), BF16),
            pltpu.VMEM((rows, BOXES), F32),
            pltpu.VMEM((GROUP, quarter, BOXES), BF16),
            pltpu.VMEM((groups, quarter, BOXES), BF16),
            pltpu.VMEM((GROUP, quarter, BOXES), BF16),
            pltpu.VMEM((padded, BOXES), BF16),
            pltpu.VMEM((NOFF * in_rows, rows), BF16),
            pltpu.VMEM((rows, lanes), BF16),
            pltpu.VMEM((4, NOFF * BOXES, 2 * BOXES), BF16),
            pltpu.VMEM((4, BOXES, BOXES), BF16),
            pltpu.VMEM((2, in_rows, NOFF * BOXES), BF16),
            pltpu.VMEM((in_rows, lanes), F32),
            pltpu.VMEM((in_rows, BOXES), F32),
            pltpu.VMEM((2, in_rows, BOXES), BF16),
            pltpu.VMEM((2, in_rows, BOXES), BF16),
            dma, dma,
            dma((GROUP,)), dma((GROUP,)),
            dma((groups,)), dma((groups,)),
            dma((GROUP,)), dma((GROUP,)),
            dma((2,)), dma((2,)),
        ],
        compiler_params=pltpu.CompilerParams(
            collective_id=0, has_side_effects=True, vmem_limit_bytes=56 * 2**20
        ),
        cost_estimate=pl.CostEstimate(
            flops=16 * rows * coeffs * lanes, bytes_accessed=6 * 2**20, transcendentals=0
        ),
    )(offsets, multipole, m2x, maps, phases, rate)
    return out[:coeffs].reshape(coeffs, layers, plane_size)


def solution(mesh):
    in_specs = (P(None, "gz", "xy"), P("gz", "xy"), P(), P(), P(), P(), P(), P())
    out_specs = P(None, "gz", "xy")
    return jax.shard_map(body, mesh=mesh, in_specs=in_specs, out_specs=out_specs, check_vma=False)
```

```python
import functools

import jax
import jax.numpy as jnp
from jax import lax
from jax.experimental import pallas as pl
from jax.experimental.pallas import tpu as pltpu
from jax.sharding import PartitionSpec as P

BY = 8
R = 2
NOFF = 6
GROUP = 4
BOXES = 128
MESH = pl.DeviceIdType.MESH
F32 = jnp.float32
BF16 = jnp.bfloat16


def up(value, step):
    return -(-value // step) * step


def kernel(
    loop_size, layers, rows,
    off_ref, moments_ref, counts_ref, m2x_ref, x2l_ref, decay_ref, wave_x_ref, wave_y_ref,
    out_ref,
    charged, poles, rates, phases, terms, outgo, top_out, top, below, ingroup, planes, entbuf,
    enter, wall, upward, total_z, perm, place, mixed, own, edge, edge_out, edge_in,
    top_s, top_r, a_s, a_r, b_s, b_r, c_s, c_r, e_s, e_r,
):
    slab = lax.axis_index("gz")
    half = lax.axis_index("xy")
    groups = loop_size // GROUP
    group, member = slab // GROUP, lax.rem(slab, GROUP)
    after = lax.rem(slab + 1, loop_size)
    before = lax.rem(slab + loop_size - 1, loop_size)
    coeffs = m2x_ref.shape[1]
    out_rows = poles.shape[0]
    parts = split_rows(rows)

    def mate(step):
        return lax.rem(member + step, GROUP)

    def mate_id(step):
        return group * GROUP + mate(step)

    def plane_id(step):
        return lax.rem(group + step, groups) * GROUP + member

    barrier = pltpu.get_barrier_semaphore()
    partners = [after, before]
    partners += [mate_id(step) for step in range(1, GROUP)]
    partners += [plane_id(step) for step in range(1, groups)]
    for partner in partners:
        pl.semaphore_signal(barrier, inc=1, device_id={"gz": partner}, device_id_type=MESH)
    pl.semaphore_signal(barrier, inc=1, device_id={"xy": 1 - half}, device_id_type=MESH)

    count = counts_ref[...].astype(F32)

    @pl.loop(0, coeffs // 8)
    def _(turn):
        part = moments_ref[pl.ds(turn * 8, 8)].astype(F32) * count[None]
        charged[pl.ds(pl.multiple_of(turn * 64, 64), 64), :] = part.reshape(64, BOXES)

    done = coeffs // 8 * 8
    part = moments_ref[done:coeffs].astype(F32) * count[None]
    charged[done * 8:coeffs * 8, :] = part.reshape((coeffs - done) * 8, BOXES)
    charged[coeffs * 8:, :] = jnp.zeros(((out_rows - coeffs) * 8, BOXES), F32)
    for z in range(layers):
        layer = charged[pl.ds(z, out_rows, stride=8), :].astype(BF16)
        poles[:, z * BOXES:(z + 1) * BOXES] = layer
        if z == layers - 1:
            top_out[...] = layer

    pl.semaphore_wait(barrier, len(partners) + 1)

    top_copy = pltpu.make_async_remote_copy(
        src_ref=top_out, dst_ref=top, send_sem=top_s, recv_sem=top_r,
        device_id={"gz": after}, device_id_type=MESH,
    )
    top_copy.start()

    decay_row = decay_ref[...]
    spare = rates.shape[0] - rows
    decay_row = jnp.concatenate([decay_row, decay_row, jnp.full((1, spare), 0.01, F32)], axis=1)
    for turn in range(rates.shape[0] // BOXES):
        at = slice(turn * BOXES, (turn + 1) * BOXES)
        rates[at, :] = jnp.transpose(jnp.broadcast_to(decay_row[:, at], (BOXES, BOXES)))

    def strip(base, turn):
        return pl.ds(pl.multiple_of(base + turn * 16, 16), 16)

    def lot(base, index, size):
        return pl.ds(pl.multiple_of(base + index * size, 16), size)

    a_copies = []
    for index, (base, size, real, inner, quarter) in enumerate(parts):
        terms[base:base + real, :] = jnp.dot(
            m2x_ref[base:base + real, :], poles[0:coeffs, :], preferred_element_type=F32)

        @pl.loop(0, real // 16)
        def _(turn):
            at = strip(base, turn)
            factor = jnp.exp(-rates[at, :])
            square = factor * factor
            weight = jnp.sqrt(1.0 - square)
            box = [weight * terms[at, z * BOXES:(z + 1) * BOXES] for z in range(layers)]
            total = box[0]
            for z in range(1, layers):
                total = factor * total + box[z]
            outgo[at, :] = total.astype(BF16)
            state = jnp.zeros_like(factor)
            for z in range(2, layers):
                state = factor * state + square * box[z - 2]
                terms[at, z * BOXES:(z + 1) * BOXES] = state

        if size > real:
            outgo[base + real:base + size, :] = jnp.zeros((size - real, BOXES), BF16)
        copies = []
        for step in range(1, GROUP):
            sem = index * GROUP + step
            copy = pltpu.make_async_remote_copy(
                src_ref=outgo.at[lot(base, mate(step), quarter), :],
                dst_ref=ingroup.at[step, pl.ds(inner, quarter), :],
                send_sem=a_s.at[sem], recv_sem=a_r.at[sem],
                device_id={"gz": mate_id(step)}, device_id_type=MESH,
            )
            copy.start()
            copies.append(copy)
        a_copies.append(copies)
        ingroup[0, inner:inner + quarter, :] = outgo[lot(base, member, quarter), :]

    row = lax.broadcasted_iota(jnp.int32, (8, rows), 0)
    side = lax.broadcasted_iota(jnp.int32, (8, rows), 1)
    step_x = jnp.zeros((8, rows), F32)
    step_y = jnp.zeros((8, rows), F32)
    for entry in range(NOFF):
        step_x = jnp.where(row == entry, off_ref[entry, 0].astype(F32), step_x)
        step_y = jnp.where(row == entry, off_ref[entry, 1].astype(F32), step_y)
    wave_x = jnp.concatenate([wave_x_ref[...], wave_x_ref[...]], axis=1)
    wave_y = jnp.concatenate([wave_y_ref[...], wave_y_ref[...]], axis=1)
    angle = wave_x * step_x + wave_y * step_y
    sine = jnp.sin(angle)
    phases[0:8, :] = jnp.cos(angle)
    phases[8:16, :] = jnp.where(side < rows // 2, sine, -sine)

    def phase_maps(x2l, place_of):
        real = x2l.astype(F32)
        swap = jnp.concatenate([real[:, rows // 2:], real[:, :rows // 2]], axis=1)
        for entry in range(NOFF):
            mix = real * phases[entry:entry + 1, :] + swap * phases[8 + entry:9 + entry, :]
            if mix.shape[0] < 16:
                mix = jnp.concatenate([mix, jnp.zeros((16 - mix.shape[0], rows), F32)], axis=0)
            wall[place_of(entry * out_rows), :] = mix.astype(BF16)

    def some_maps(low, high):
        @pl.loop(low, high)
        def _(turn):
            phase_maps(x2l_ref[strip(0, turn), :], lambda base: strip(base, turn))

    def send_planes(index):
        base, size, real, inner, quarter = parts[index]
        for copy in a_copies[index]:
            copy.wait_recv()
        decay = jnp.exp(-rates[lot(base, member, quarter), :] * layers)
        total = source(0, index)
        for other in range(1, GROUP):
            total = decay * total + source(other, index)
        planes[0, inner:inner + quarter, :] = total.astype(BF16)
        copies = []
        for step in range(1, groups):
            sem = index * groups + step
            copy = pltpu.make_async_remote_copy(
                src_ref=planes.at[0, pl.ds(inner, quarter), :],
                dst_ref=planes.at[step, pl.ds(inner, quarter), :],
                send_sem=b_s.at[sem], recv_sem=b_r.at[sem],
                device_id={"gz": plane_id(step)}, device_id_type=MESH,
            )
            copy.start()
            copies.append(copy)
        return copies

    def source(other, index):
        base, size, real, inner, quarter = parts[index]
        return ingroup[lax.rem(member - other + GROUP, GROUP), inner:inner + quarter, :].astype(F32)

    def send_entering(index):
        base, size, real, inner, quarter = parts[index]
        for copy in b_copies[index]:
            copy.wait_recv()
        at = slice(inner, inner + quarter)
        rate = rates[lot(base, member, quarter), :]
        decay = jnp.exp(-rate * layers)
        plane_decay = jnp.exp(-rate * (layers * GROUP))
        total = planes[0, at, :].astype(F32)
        for step in range(groups - 1, 0, -1):
            total = plane_decay * total + planes[step, at, :].astype(F32)
        state = total / (1.0 - jnp.exp(-rate * (layers * loop_size)))
        entbuf[0, at, :] = state.astype(BF16)
        for other in range(1, GROUP):
            state = decay * state + source(other - 1, index)
            entbuf[other, at, :] = state.astype(BF16)
        copies = []
        for step in range(1, GROUP):
            sem = index * GROUP + step
            copy = pltpu.make_async_remote_copy(
                src_ref=entbuf.at[mate(step), pl.ds(inner, quarter), :],
                dst_ref=enter.at[lot(base, member, quarter), :],
                send_sem=c_s.at[sem], recv_sem=c_r.at[sem],
                device_id={"gz": mate_id(step)}, device_id_type=MESH,
            )
            copy.start()
            copies.append(copy)
        enter[lot(base, member, quarter), :] = entbuf[member, at, :]
        return copies

    def raise_part(index):
        base, size, real, inner, quarter = parts[index]
        for step in range(1, GROUP):
            sem = index * GROUP + step
            sender = lax.rem(member - step + GROUP, GROUP)
            pltpu.make_async_remote_copy(
                src_ref=entbuf.at[0, pl.ds(inner, quarter), :],
                dst_ref=enter.at[lot(base, sender, quarter), :],
                send_sem=c_s.at[sem], recv_sem=c_r.at[sem],
                device_id={"gz": mate_id(step)}, device_id_type=MESH,
            ).wait_recv()

        @pl.loop(0, real // 16)
        def _(turn):
            at = strip(base, turn)
            factor = jnp.exp(-rates[at, :])
            weight = jnp.sqrt(1.0 - factor * factor)
            state = factor * enter[at, :].astype(F32)
            upward[at, 0:BOXES] = (state - factor * (weight * below[at, :])).astype(BF16)
            state = factor * state
            upward[at, BOXES:2 * BOXES] = state.astype(BF16)
            for z in range(2, layers):
                state = factor * state
                upward[at, z * BOXES:(z + 1) * BOXES] = (
                    state + terms[at, z * BOXES:(z + 1) * BOXES]).astype(BF16)

    def map_part(index, entry, pair):
        base, size, real, inner, quarter = parts[index]
        two = pl.multiple_of(pair * 2 * BOXES, 2 * BOXES)
        return jnp.dot(
            wall[pl.ds(pl.multiple_of(entry * 2 * out_rows, 16), 2 * out_rows), base:base + real],
            upward[base:base + real, pl.ds(two, 2 * BOXES)],
            preferred_element_type=F32)

    def add_part(index):
        @pl.loop(0, layers // 2)
        def _(pair):
            @pl.loop(0, NOFF // 2)
            def _(entry):
                if index == 0:
                    total_z[pair, entry] = map_part(index, entry, pair)
                else:
                    total_z[pair, entry] += map_part(index, entry, pair)

    full = coeffs // 16
    b_copies = [send_planes(0)]
    some_maps(0, full // 2)
    b_copies.append(send_planes(1))
    some_maps(full // 2, full)
    phase_maps(x2l_ref[full * 16:coeffs, :], lambda base: pl.ds(base + full * 16, 16))
    b_copies.append(send_planes(2))

    lane = lax.broadcasted_iota(jnp.int32, (BOXES, 2 * BOXES), 0)
    column = lax.broadcasted_iota(jnp.int32, (BOXES, 2 * BOXES), 1)
    width = BOXES // BY
    for entry in range(NOFF):
        moved_x = lane // BY + off_ref[entry, 0]
        moved_y = (lane + off_ref[entry, 1]) & (BY - 1)
        inside = moved_x * BY + moved_y
        low = (moved_x + R) * BY + moved_y + BOXES
        high = (moved_x - width + R) * BY + moved_y + BOXES
        stays = (moved_x >= 0) & (moved_x < width)
        outside = jnp.where(moved_x < 0, low, high)
        for slot in range(4):
            target = jnp.where(stays, inside, outside + slot * 2 * R * BY)
            perm[slot, entry * BOXES:(entry + 1) * BOXES, :] = jnp.where(
                column == target, 1.0, 0.0).astype(BF16)
    lane = lax.broadcasted_iota(jnp.int32, (BOXES, BOXES), 0)
    column = lax.broadcasted_iota(jnp.int32, (BOXES, BOXES), 1)
    for slot in range(4):
        inner = lane - slot * 2 * R * BY
        target = jnp.where(inner < R * BY, inner + BOXES - R * BY, inner - R * BY)
        hit = (inner >= 0) & (inner < 2 * R * BY) & (column == target)
        place[slot] = jnp.where(hit, 1.0, 0.0).astype(BF16)

    top_copy.wait_recv()
    below[...] = jnp.dot(m2x_ref[...], top[0:coeffs, :], preferred_element_type=F32)

    c_copies = [send_entering(0), send_entering(1)]
    raise_part(0)
    c_copies.append(send_entering(2))
    add_part(0)
    raise_part(1)
    add_part(1)
    raise_part(2)

    e_copies = []
    for pair in range(layers // 2):
        for entry in range(NOFF // 2):
            part = (total_z[pair, entry] + map_part(2, entry, pair)).astype(BF16)
            for which in range(2):
                at = slice((entry * 2 + which) * BOXES, (entry * 2 + which + 1) * BOXES)
                mine = part[which * out_rows:(which + 1) * out_rows]
                mixed[0, :, at] = mine[:, :BOXES]
                mixed[1, :, at] = mine[:, BOXES:]

        for inner in range(2):
            z = pair * 2 + inner
            placed = jnp.dot(mixed[inner], perm[z % 4], preferred_element_type=F32)
            own[:, z * BOXES:(z + 1) * BOXES] = placed[:, :BOXES]
            if z % 4 == 0:
                edge[...] = placed[:, BOXES:]
            else:
                edge[...] += placed[:, BOXES:]
        if pair % 2 == 1:
            side = pair // 2
            edge_out[side] = edge[...].astype(BF16)
            copy = pltpu.make_async_remote_copy(
                src_ref=edge_out.at[side], dst_ref=edge_in.at[side],
                send_sem=e_s.at[side], recv_sem=e_r.at[side],
                device_id={"xy": 1 - half}, device_id_type=MESH,
            )
            copy.start()
            e_copies.append(copy)

    for side, copy in enumerate(e_copies):
        copy.wait_recv()
        for slot in range(4):
            at = slice((side * 4 + slot) * BOXES, (side * 4 + slot + 1) * BOXES)
            out_ref[:, at] = (
                own[:, at] + jnp.dot(edge_in[side], place[slot], preferred_element_type=F32)
            ).astype(BF16)[:coeffs]

    sent = [top_copy] + e_copies
    for copies in a_copies + b_copies + c_copies:
        sent += copies
    for copy in sent:
        copy.wait_send()


def split_rows(rows):
    first = up(rows // 3, BOXES)
    parts, base, inner = [], 0, 0
    while base < rows:
        real = min(first, rows - base)
        size = up(real, 16 * GROUP)
        parts.append((base, size, real, inner, size // GROUP))
        base, inner = base + real, inner + size // GROUP
    return parts


def body(moments, counts, m2x, x2l, decay_rate, wave_x, wave_y, offsets):
    coeffs, layers, plane_size = moments.shape
    rows = m2x.shape[0]
    loop_size = lax.axis_size("gz")
    groups = loop_size // GROUP
    parts = split_rows(rows)
    padded = parts[-1][0] + parts[-1][1]
    quarter = parts[-1][3] + parts[-1][4]
    count = len(parts)
    in_rows = up(coeffs, 16)
    lanes = layers * plane_size

    vmem = pl.BlockSpec(memory_space=pltpu.VMEM)
    dma = pltpu.SemaphoreType.DMA
    out = pl.pallas_call(
        functools.partial(kernel, loop_size, layers, rows),
        out_shape=jax.ShapeDtypeStruct((coeffs, lanes), BF16),
        in_specs=[pl.BlockSpec(memory_space=pltpu.SMEM)] + [vmem] * 7,
        out_specs=vmem,
        scratch_shapes=[
            pltpu.VMEM((in_rows * 8, BOXES), F32),
            pltpu.VMEM((in_rows, lanes), BF16),
            pltpu.VMEM((up(padded, BOXES), BOXES), F32),
            pltpu.VMEM((16, rows), F32),
            pltpu.VMEM((rows, lanes), F32),
            pltpu.VMEM((padded, BOXES), BF16),
            pltpu.VMEM((in_rows, BOXES), BF16),
            pltpu.VMEM((in_rows, BOXES), BF16),
            pltpu.VMEM((rows, BOXES), F32),
            pltpu.VMEM((GROUP, quarter, BOXES), BF16),
            pltpu.VMEM((groups, quarter, BOXES), BF16),
            pltpu.VMEM((GROUP, quarter, BOXES), BF16),
            pltpu.VMEM((padded, BOXES), BF16),
            pltpu.VMEM((NOFF * in_rows, rows), BF16),
            pltpu.VMEM((rows, lanes), BF16),
            pltpu.VMEM((layers // 2, NOFF // 2, 2 * in_rows, 2 * BOXES), F32),
            pltpu.VMEM((4, NOFF * BOXES, 2 * BOXES), BF16),
            pltpu.VMEM((4, BOXES, BOXES), BF16),
            pltpu.VMEM((2, in_rows, NOFF * BOXES), BF16),
            pltpu.VMEM((in_rows, lanes), F32),
            pltpu.VMEM((in_rows, BOXES), F32),
            pltpu.VMEM((2, in_rows, BOXES), BF16),
            pltpu.VMEM((2, in_rows, BOXES), BF16),
            dma, dma,
            dma((count * GROUP,)), dma((count * GROUP,)),
            dma((count * groups,)), dma((count * groups,)),
            dma((count * GROUP,)), dma((count * GROUP,)),
            dma((2,)), dma((2,)),
        ],
        compiler_params=pltpu.CompilerParams(
            collective_id=0, has_side_effects=True, vmem_limit_bytes=58 * 2**20
        ),
        cost_estimate=pl.CostEstimate(
            flops=16 * rows * coeffs * lanes, bytes_accessed=6 * 2**20, transcendentals=0
        ),
    )(offsets, moments, counts, m2x, x2l, decay_rate[None], wave_x[None], wave_y[None])
    return out.reshape(coeffs, layers, plane_size)


def solution(mesh):
    in_specs = (P(None, "gz", "xy"), P("gz", "xy"), P(), P(), P(), P(), P(), P())
    out_specs = P(None, "gz", "xy")
    return jax.shard_map(body, mesh=mesh, in_specs=in_specs, out_specs=out_specs, check_vma=False)
```

```python
import functools

import jax
import jax.numpy as jnp
from jax import lax
from jax.experimental import pallas as pl
from jax.experimental.pallas import tpu as pltpu
from jax.sharding import PartitionSpec as P

BY = 8
R = 2
NOFF = 6
GROUP = 4
BOXES = 128
MESH = pl.DeviceIdType.MESH
F32 = jnp.float32
BF16 = jnp.bfloat16


def up(value, step):
    return -(-value // step) * step


def kernel(
    loop_size, layers, rows,
    off_ref, moments_ref, counts_ref, m2x_ref, x2l_ref, decay_ref, wave_x_ref, wave_y_ref,
    out_ref,
    charged, poles, rates, factors, weights, spread, phases, terms, outgo, top_out, top, below, ingroup, planes, entbuf,
    enter, wall, upward, total_z, perm, place, mixed, own, edge, edge_out, edge_in,
    top_s, top_r, a_s, a_r, b_s, b_r, c_s, c_r, e_s, e_r,
):
    slab = lax.axis_index("gz")
    half = lax.axis_index("xy")
    groups = loop_size // GROUP
    group, member = slab // GROUP, lax.rem(slab, GROUP)
    after = lax.rem(slab + 1, loop_size)
    before = lax.rem(slab + loop_size - 1, loop_size)
    coeffs = m2x_ref.shape[1]
    out_rows = poles.shape[0]
    parts = split_rows(rows)

    def mate(step):
        return lax.rem(member + step, GROUP)

    def mate_id(step):
        return group * GROUP + mate(step)

    def plane_id(step):
        return lax.rem(group + step, groups) * GROUP + member

    barrier = pltpu.get_barrier_semaphore()
    partners = [after, before]
    partners += [mate_id(step) for step in range(1, GROUP)]
    partners += [plane_id(step) for step in range(1, groups)]
    for partner in partners:
        pl.semaphore_signal(barrier, inc=1, device_id={"gz": partner}, device_id_type=MESH)
    pl.semaphore_signal(barrier, inc=1, device_id={"xy": 1 - half}, device_id_type=MESH)

    count = counts_ref[...].astype(F32)

    @pl.loop(0, coeffs // 8)
    def _(turn):
        part = moments_ref[pl.ds(turn * 8, 8)].astype(F32) * count[None]
        charged[pl.ds(pl.multiple_of(turn * 64, 64), 64), :] = part.reshape(64, BOXES)

    done = coeffs // 8 * 8
    part = moments_ref[done:coeffs].astype(F32) * count[None]
    charged[done * 8:coeffs * 8, :] = part.reshape((coeffs - done) * 8, BOXES)
    charged[coeffs * 8:, :] = jnp.zeros(((out_rows - coeffs) * 8, BOXES), F32)
    for z in range(layers):
        layer = charged[pl.ds(z, out_rows, stride=8), :].astype(BF16)
        poles[:, z * BOXES:(z + 1) * BOXES] = layer
        if z == layers - 1:
            top_out[...] = layer

    long_rows = rates.shape[0]
    spare = long_rows - rows
    decay_row = decay_ref[...].reshape(1, rows // 2)
    decay_row = jnp.concatenate([decay_row, decay_row, jnp.full((1, spare), 0.01, F32)], axis=1)
    for turn in range(long_rows // BOXES):
        at = slice(turn * BOXES, (turn + 1) * BOXES)
        rate = jnp.transpose(jnp.broadcast_to(decay_row[:, at], (BOXES, BOXES)))
        factor = jnp.exp(-rate)
        rates[at, :] = rate
        factors[at, :] = factor
        weights[at, :] = jnp.sqrt(1.0 - factor * factor)

    pl.semaphore_wait(barrier, len(partners) + 1)

    top_copy = pltpu.make_async_remote_copy(
        src_ref=top_out, dst_ref=top, send_sem=top_s, recv_sem=top_r,
        device_id={"gz": after}, device_id_type=MESH,
    )
    top_copy.start()

    def strips(base, real, work):
        @pl.loop(0, real // 32)
        def _(turn):
            work(pl.ds(pl.multiple_of(base + turn * 32, 32), 32))

        if real % 32:
            work(pl.ds(base + real // 32 * 32, real % 32))

    def lot(base, index, size):
        return pl.ds(pl.multiple_of(base + index * size, 16), size)

    a_copies = []
    for index, (base, size, real, inner, quarter) in enumerate(parts):
        terms[base:base + real, :] = jnp.dot(
            m2x_ref[base:base + real, :], poles[0:coeffs, :], preferred_element_type=F32)

        def fold(at):
            factor, weight = factors[at, :], weights[at, :]
            square = factor * factor
            older = old = None
            for z in range(layers):
                box = weight * terms[at, z * BOXES:(z + 1) * BOXES]
                total = box if z == 0 else factor * total + box
                if z >= 2:
                    state = square * older if z == 2 else factor * state + square * older
                    terms[at, z * BOXES:(z + 1) * BOXES] = state
                older, old = old, box
            outgo[at, :] = total.astype(BF16)

        strips(base, real, fold)
        if size > real:
            outgo[base + real:base + size, :] = jnp.zeros((size - real, BOXES), BF16)
        copies = []
        for step in range(1, GROUP):
            sem = index * GROUP + step
            copy = pltpu.make_async_remote_copy(
                src_ref=outgo.at[lot(base, mate(step), quarter), :],
                dst_ref=ingroup.at[step, pl.ds(inner, quarter), :],
                send_sem=a_s.at[sem], recv_sem=a_r.at[sem],
                device_id={"gz": mate_id(step)}, device_id_type=MESH,
            )
            copy.start()
            copies.append(copy)
        a_copies.append(copies)
        ingroup[0, inner:inner + quarter, :] = outgo[lot(base, member, quarter), :]

    row = lax.broadcasted_iota(jnp.int32, (8, long_rows), 0)
    side = lax.broadcasted_iota(jnp.int32, (8, long_rows), 1)
    step_x = jnp.zeros((8, long_rows), F32)
    step_y = jnp.zeros((8, long_rows), F32)
    for entry in range(NOFF):
        step_x = jnp.where(row == entry, off_ref[0, entry].astype(F32), step_x)
        step_y = jnp.where(row == entry, off_ref[1, entry].astype(F32), step_y)
    gap = jnp.zeros((1, spare), F32)
    wave_x = wave_x_ref[...].reshape(1, rows // 2)
    wave_y = wave_y_ref[...].reshape(1, rows // 2)
    wave_x = jnp.concatenate([wave_x, wave_x, gap], axis=1)
    wave_y = jnp.concatenate([wave_y, wave_y, gap], axis=1)
    angle = wave_x * step_x + wave_y * step_y
    sine = jnp.sin(angle)
    phases[0:8, :] = jnp.cos(angle)
    phases[8:16, :] = jnp.where(side < rows // 2, sine, -sine)
    spread[:, up(coeffs, BOXES) - BOXES:] = jnp.zeros((long_rows, BOXES), F32)
    spread[rows:, :] = jnp.zeros((spare, up(coeffs, BOXES)), F32)
    spread[0:rows, 0:coeffs] = x2l_ref[...].astype(F32)

    def some_maps(low, high):
        for turn in range(low, high):
            at = slice(turn * BOXES, (turn + 1) * BOXES)
            start = (turn * BOXES + rows // 2) % rows
            if start + BOXES <= rows:
                swap = spread[start:start + BOXES, :]
            else:
                swap = jnp.concatenate(
                    [spread[start:rows, :], spread[0:start + BOXES - rows, :]], axis=0)
            real = jnp.transpose(spread[at, :])[:out_rows]
            swap = jnp.transpose(swap)[:out_rows]
            for entry in range(NOFF):
                mix = real * phases[entry:entry + 1, at] + swap * phases[8 + entry:9 + entry, at]
                wall[entry * out_rows:(entry + 1) * out_rows, at] = mix.astype(BF16)

    def send_planes(index):
        base, size, real, inner, quarter = parts[index]
        for copy in a_copies[index]:
            copy.wait_recv()
        decay = jnp.exp(-rates[lot(base, member, quarter), :] * layers)
        total = source(0, index)
        for other in range(1, GROUP):
            total = decay * total + source(other, index)
        planes[0, inner:inner + quarter, :] = total.astype(BF16)
        copies = []
        for step in range(1, groups):
            sem = index * groups + step
            copy = pltpu.make_async_remote_copy(
                src_ref=planes.at[0, pl.ds(inner, quarter), :],
                dst_ref=planes.at[step, pl.ds(inner, quarter), :],
                send_sem=b_s.at[sem], recv_sem=b_r.at[sem],
                device_id={"gz": plane_id(step)}, device_id_type=MESH,
            )
            copy.start()
            copies.append(copy)
        return copies

    def source(other, index):
        base, size, real, inner, quarter = parts[index]
        return ingroup[lax.rem(member - other + GROUP, GROUP), inner:inner + quarter, :].astype(F32)

    def send_entering(index):
        base, size, real, inner, quarter = parts[index]
        for copy in b_copies[index]:
            copy.wait_recv()
        at = slice(inner, inner + quarter)
        rate = rates[lot(base, member, quarter), :]
        decay = jnp.exp(-rate * layers)
        plane_decay = jnp.exp(-rate * (layers * GROUP))
        total = planes[0, at, :].astype(F32)
        for step in range(groups - 1, 0, -1):
            total = plane_decay * total + planes[step, at, :].astype(F32)
        state = total / (1.0 - jnp.exp(-rate * (layers * loop_size)))
        entbuf[0, at, :] = state.astype(BF16)
        for other in range(1, GROUP):
            state = decay * state + source(other - 1, index)
            entbuf[other, at, :] = state.astype(BF16)
        copies = []
        for step in range(1, GROUP):
            sem = index * GROUP + step
            copy = pltpu.make_async_remote_copy(
                src_ref=entbuf.at[mate(step), pl.ds(inner, quarter), :],
                dst_ref=enter.at[lot(base, member, quarter), :],
                send_sem=c_s.at[sem], recv_sem=c_r.at[sem],
                device_id={"gz": mate_id(step)}, device_id_type=MESH,
            )
            copy.start()
            copies.append(copy)
        enter[lot(base, member, quarter), :] = entbuf[member, at, :]
        return copies

    def raise_part(index):
        base, size, real, inner, quarter = parts[index]
        for step in range(1, GROUP):
            sem = index * GROUP + step
            sender = lax.rem(member - step + GROUP, GROUP)
            pltpu.make_async_remote_copy(
                src_ref=entbuf.at[0, pl.ds(inner, quarter), :],
                dst_ref=enter.at[lot(base, sender, quarter), :],
                send_sem=c_s.at[sem], recv_sem=c_r.at[sem],
                device_id={"gz": mate_id(step)}, device_id_type=MESH,
            ).wait_recv()

        def lift(at):
            factor = factors[at, :]
            state = factor * enter[at, :].astype(F32)
            upward[at, 0:BOXES] = (state - factor * (weights[at, :] * below[at, :])).astype(BF16)
            state = factor * state
            upward[at, BOXES:2 * BOXES] = state.astype(BF16)
            for z in range(2, layers):
                state = factor * state
                upward[at, z * BOXES:(z + 1) * BOXES] = (
                    state + terms[at, z * BOXES:(z + 1) * BOXES]).astype(BF16)

        strips(base, real, lift)

    def map_part(index, entry, pair):
        base, size, real, inner, quarter = parts[index]
        two = pl.multiple_of(pair * 2 * BOXES, 2 * BOXES)
        return jnp.dot(
            wall[pl.ds(pl.multiple_of(entry * 2 * out_rows, 16), 2 * out_rows), base:base + real],
            upward[base:base + real, pl.ds(two, 2 * BOXES)],
            preferred_element_type=F32)

    def add_part(index):
        @pl.loop(0, layers // 2)
        def _(pair):
            @pl.loop(0, NOFF // 2)
            def _(entry):
                if index == 0:
                    total_z[pair, entry] = map_part(index, entry, pair)
                else:
                    total_z[pair, entry] += map_part(index, entry, pair)

    turns = long_rows // BOXES
    b_copies = [send_planes(0)]
    some_maps(0, turns // 2)
    b_copies.append(send_planes(1))
    some_maps(turns // 2, turns)
    b_copies.append(send_planes(2))

    lane = lax.broadcasted_iota(jnp.int32, (BOXES, 2 * BOXES), 0)
    column = lax.broadcasted_iota(jnp.int32, (BOXES, 2 * BOXES), 1)
    width = BOXES // BY
    for entry in range(NOFF):
        moved_x = lane // BY + off_ref[0, entry]
        moved_y = (lane + off_ref[1, entry]) & (BY - 1)
        inside = moved_x * BY + moved_y
        low = (moved_x + R) * BY + moved_y + BOXES
        high = (moved_x - width + R) * BY + moved_y + BOXES
        stays = (moved_x >= 0) & (moved_x < width)
        outside = jnp.where(moved_x < 0, low, high)
        for slot in range(4):
            target = jnp.where(stays, inside, outside + slot * 2 * R * BY)
            perm[slot, entry * BOXES:(entry + 1) * BOXES, :] = jnp.where(
                column == target, 1.0, 0.0).astype(BF16)
    lane = lax.broadcasted_iota(jnp.int32, (BOXES, BOXES), 0)
    column = lax.broadcasted_iota(jnp.int32, (BOXES, BOXES), 1)
    for slot in range(4):
        inner = lane - slot * 2 * R * BY
        target = jnp.where(inner < R * BY, inner + BOXES - R * BY, inner - R * BY)
        hit = (inner >= 0) & (inner < 2 * R * BY) & (column == target)
        place[slot] = jnp.where(hit, 1.0, 0.0).astype(BF16)

    top_copy.wait_recv()
    below[...] = jnp.dot(m2x_ref[...], top[0:coeffs, :], preferred_element_type=F32)

    c_copies = [send_entering(0), send_entering(1)]
    raise_part(0)
    c_copies.append(send_entering(2))
    add_part(0)
    raise_part(1)
    add_part(1)
    raise_part(2)

    e_copies = []
    for pair in range(layers // 2):
        for entry in range(NOFF // 2):
            part = (total_z[pair, entry] + map_part(2, entry, pair)).astype(BF16)
            for which in range(2):
                at = slice((entry * 2 + which) * BOXES, (entry * 2 + which + 1) * BOXES)
                mine = part[which * out_rows:(which + 1) * out_rows]
                mixed[0, :, at] = mine[:, :BOXES]
                mixed[1, :, at] = mine[:, BOXES:]

        for inner in range(2):
            z = pair * 2 + inner
            placed = jnp.dot(mixed[inner], perm[z % 4], preferred_element_type=F32)
            own[:, z * BOXES:(z + 1) * BOXES] = placed[:, :BOXES]
            if z % 4 == 0:
                edge[...] = placed[:, BOXES:]
            else:
                edge[...] += placed[:, BOXES:]
        if pair % 2 == 1:
            side = pair // 2
            edge_out[side] = edge[...].astype(BF16)
            copy = pltpu.make_async_remote_copy(
                src_ref=edge_out.at[side], dst_ref=edge_in.at[side],
                send_sem=e_s.at[side], recv_sem=e_r.at[side],
                device_id={"xy": 1 - half}, device_id_type=MESH,
            )
            copy.start()
            e_copies.append(copy)

    for side, copy in enumerate(e_copies):
        copy.wait_recv()
        for slot in range(4):
            at = slice((side * 4 + slot) * BOXES, (side * 4 + slot + 1) * BOXES)
            charged[pl.ds(side * 4 + slot, out_rows, stride=8), :] = (
                own[:, at] + jnp.dot(edge_in[side], place[slot], preferred_element_type=F32))

    @pl.loop(0, coeffs // 8)
    def _(turn):
        part = charged[pl.ds(pl.multiple_of(turn * 64, 64), 64), :]
        out_ref[pl.ds(turn * 8, 8)] = part.reshape(8, 8, BOXES).astype(BF16)

    out_ref[done:coeffs] = charged[done * 8:coeffs * 8, :].reshape(
        coeffs - done, 8, BOXES).astype(BF16)

    sent = [top_copy] + e_copies
    for copies in a_copies + b_copies + c_copies:
        sent += copies
    for copy in sent:
        copy.wait_send()


def split_rows(rows):
    first = up(rows // 3, BOXES)
    parts, base, inner = [], 0, 0
    for wanted in (first, first + BOXES, rows):
        real = min(wanted, rows - base)
        size = up(real, 16 * GROUP)
        parts.append((base, size, real, inner, size // GROUP))
        base, inner = base + real, inner + size // GROUP
    return parts


def body(moments, counts, m2x, x2l, decay_rate, wave_x, wave_y, offsets):
    coeffs, layers, plane_size = moments.shape
    rows = m2x.shape[0]
    loop_size = lax.axis_size("gz")
    groups = loop_size // GROUP
    parts = split_rows(rows)
    padded = parts[-1][0] + parts[-1][1]
    quarter = parts[-1][3] + parts[-1][4]
    count = len(parts)
    in_rows = up(coeffs, 16)
    long_rows = up(padded, BOXES)
    lanes = layers * plane_size

    vmem = pl.BlockSpec(memory_space=pltpu.VMEM)
    dma = pltpu.SemaphoreType.DMA
    return pl.pallas_call(
        functools.partial(kernel, loop_size, layers, rows),
        out_shape=jax.ShapeDtypeStruct(moments.shape, BF16),
        in_specs=[pl.BlockSpec(memory_space=pltpu.SMEM)] + [vmem] * 7,
        out_specs=vmem,
        scratch_shapes=[
            pltpu.VMEM((in_rows * 8, BOXES), F32),
            pltpu.VMEM((in_rows, lanes), BF16),
            pltpu.VMEM((long_rows, BOXES), F32),
            pltpu.VMEM((long_rows, BOXES), F32),
            pltpu.VMEM((long_rows, BOXES), F32),
            pltpu.VMEM((long_rows, up(coeffs, BOXES)), F32),
            pltpu.VMEM((16, long_rows), F32),
            pltpu.VMEM((rows, lanes), F32),
            pltpu.VMEM((padded, BOXES), BF16),
            pltpu.VMEM((in_rows, BOXES), BF16),
            pltpu.VMEM((in_rows, BOXES), BF16),
            pltpu.VMEM((rows, BOXES), F32),
            pltpu.VMEM((GROUP, quarter, BOXES), BF16),
            pltpu.VMEM((groups, quarter, BOXES), BF16),
            pltpu.VMEM((GROUP, quarter, BOXES), BF16),
            pltpu.VMEM((padded, BOXES), BF16),
            pltpu.VMEM((NOFF * in_rows, long_rows), BF16),
            pltpu.VMEM((rows, lanes), BF16),
            pltpu.VMEM((layers // 2, NOFF // 2, 2 * in_rows, 2 * BOXES), F32),
            pltpu.VMEM((4, NOFF * BOXES, 2 * BOXES), BF16),
            pltpu.VMEM((4, BOXES, BOXES), BF16),
            pltpu.VMEM((2, in_rows, NOFF * BOXES), BF16),
            pltpu.VMEM((in_rows, lanes), F32),
            pltpu.VMEM((in_rows, BOXES), F32),
            pltpu.VMEM((2, in_rows, BOXES), BF16),
            pltpu.VMEM((2, in_rows, BOXES), BF16),
            dma, dma,
            dma((count * GROUP,)), dma((count * GROUP,)),
            dma((count * groups,)), dma((count * groups,)),
            dma((count * GROUP,)), dma((count * GROUP,)),
            dma((2,)), dma((2,)),
        ],
        compiler_params=pltpu.CompilerParams(
            collective_id=0, has_side_effects=True, vmem_limit_bytes=58 * 2**20
        ),
        cost_estimate=pl.CostEstimate(
            flops=16 * rows * coeffs * lanes, bytes_accessed=6 * 2**20, transcendentals=0
        ),
    )(offsets.T, moments, counts, m2x, x2l.T, decay_rate, wave_x, wave_y)


def solution(mesh):
    in_specs = (P(None, "gz", "xy"), P("gz", "xy"), P(), P(), P(), P(), P(), P())
    out_specs = P(None, "gz", "xy")
    return jax.shard_map(body, mesh=mesh, in_specs=in_specs, out_specs=out_specs, check_vma=False)
```

```python
import functools

import jax
import jax.numpy as jnp
from jax import lax
from jax.experimental import pallas as pl
from jax.experimental.pallas import tpu as pltpu
from jax.sharding import PartitionSpec as P

BY = 8
R = 2
NOFF = 6
GROUP = 4
BOXES = 128
MESH = pl.DeviceIdType.MESH
F32 = jnp.float32
BF16 = jnp.bfloat16


def up(value, step):
    return -(-value // step) * step


def kernel(
    loop_size, layers, rows,
    off_ref, moments_ref, counts_ref, m2x_ref, x2l_ref, decay_ref, wave_x_ref, wave_y_ref,
    out_ref,
    charged, poles, rates, factors, weights, spread, phases, terms, outgo, top_out, top, below, ingroup, planes, entbuf,
    enter, wall, upward, total_z, perm, place, mixed, own, edge, edge_out, edge_in,
    top_s, top_r, a_s, a_r, b_s, b_r, c_s, c_r, e_s, e_r,
):
    slab = lax.axis_index("gz")
    half = lax.axis_index("xy")
    groups = loop_size // GROUP
    group, member = slab // GROUP, lax.rem(slab, GROUP)
    after = lax.rem(slab + 1, loop_size)
    before = lax.rem(slab + loop_size - 1, loop_size)
    coeffs = m2x_ref.shape[1]
    out_rows = poles.shape[0]
    parts = split_rows(rows)

    def mate(step):
        return lax.rem(member + step, GROUP)

    def mate_id(step):
        return group * GROUP + mate(step)

    def plane_id(step):
        return lax.rem(group + step, groups) * GROUP + member

    barrier = pltpu.get_barrier_semaphore()
    partners = [after, before]
    partners += [mate_id(step) for step in range(1, GROUP)]
    partners += [plane_id(step) for step in range(1, groups)]
    for partner in partners:
        pl.semaphore_signal(barrier, inc=1, device_id={"gz": partner}, device_id_type=MESH)
    pl.semaphore_signal(barrier, inc=1, device_id={"xy": 1 - half}, device_id_type=MESH)

    count = counts_ref[...].astype(F32)

    @pl.loop(0, coeffs // 8)
    def _(turn):
        part = moments_ref[pl.ds(turn * 8, 8)].astype(F32) * count[None]
        charged[pl.ds(pl.multiple_of(turn * 64, 64), 64), :] = part.reshape(64, BOXES)

    done = coeffs // 8 * 8
    part = moments_ref[done:coeffs].astype(F32) * count[None]
    charged[done * 8:coeffs * 8, :] = part.reshape((coeffs - done) * 8, BOXES)
    charged[coeffs * 8:, :] = jnp.zeros(((out_rows - coeffs) * 8, BOXES), F32)
    for z in range(layers):
        layer = charged[pl.ds(z, out_rows, stride=8), :].astype(BF16)
        poles[:, z * BOXES:(z + 1) * BOXES] = layer
        if z == layers - 1:
            top_out[...] = layer

    long_rows = rates.shape[0]
    spare = long_rows - rows
    decay_row = decay_ref[...].reshape(1, rows // 2)
    decay_row = jnp.concatenate([decay_row, decay_row, jnp.full((1, spare), 0.01, F32)], axis=1)
    for turn in range(long_rows // BOXES):
        at = slice(turn * BOXES, (turn + 1) * BOXES)
        rate = jnp.transpose(jnp.broadcast_to(decay_row[:, at], (BOXES, BOXES)))
        factor = jnp.exp(-rate)
        rates[at, :] = rate
        factors[at, :] = factor
        weights[at, :] = jnp.sqrt(1.0 - factor * factor)

    pl.semaphore_wait(barrier, len(partners) + 1)

    top_copy = pltpu.make_async_remote_copy(
        src_ref=top_out, dst_ref=top, send_sem=top_s, recv_sem=top_r,
        device_id={"gz": after}, device_id_type=MESH,
    )
    top_copy.start()

    def strips(base, real, work):
        @pl.loop(0, real // 32)
        def _(turn):
            work(pl.ds(pl.multiple_of(base + turn * 32, 32), 32))

        if real % 32:
            work(pl.ds(base + real // 32 * 32, real % 32))

    def lot(base, index, size):
        return pl.ds(pl.multiple_of(base + index * size, 16), size)

    a_copies = []
    for index, (base, size, real, inner, quarter) in enumerate(parts):
        terms[base:base + real, :] = jnp.dot(
            m2x_ref[base:base + real, :], poles[0:coeffs, :], preferred_element_type=F32)

        def fold(at):
            factor, weight = factors[at, :], weights[at, :]
            square = factor * factor
            older = old = None
            for z in range(layers):
                box = weight * terms[at, z * BOXES:(z + 1) * BOXES]
                total = box if z == 0 else factor * total + box
                if z >= 2:
                    state = square * older if z == 2 else factor * state + square * older
                    terms[at, z * BOXES:(z + 1) * BOXES] = state
                older, old = old, box
            outgo[at, :] = total.astype(BF16)

        strips(base, real, fold)
        if size > real:
            outgo[base + real:base + size, :] = jnp.zeros((size - real, BOXES), BF16)
        copies = []
        for step in range(1, GROUP):
            sem = index * GROUP + step
            copy = pltpu.make_async_remote_copy(
                src_ref=outgo.at[lot(base, mate(step), quarter), :],
                dst_ref=ingroup.at[step, pl.ds(inner, quarter), :],
                send_sem=a_s.at[sem], recv_sem=a_r.at[sem],
                device_id={"gz": mate_id(step)}, device_id_type=MESH,
            )
            copy.start()
            copies.append(copy)
        a_copies.append(copies)
        ingroup[0, inner:inner + quarter, :] = outgo[lot(base, member, quarter), :]

    row = lax.broadcasted_iota(jnp.int32, (8, long_rows), 0)
    side = lax.broadcasted_iota(jnp.int32, (8, long_rows), 1)
    step_x = jnp.zeros((8, long_rows), F32)
    step_y = jnp.zeros((8, long_rows), F32)
    for entry in range(NOFF):
        step_x = jnp.where(row == entry, off_ref[0, entry].astype(F32), step_x)
        step_y = jnp.where(row == entry, off_ref[1, entry].astype(F32), step_y)
    gap = jnp.zeros((1, spare), F32)
    wave_x = wave_x_ref[...].reshape(1, rows // 2)
    wave_y = wave_y_ref[...].reshape(1, rows // 2)
    wave_x = jnp.concatenate([wave_x, wave_x, gap], axis=1)
    wave_y = jnp.concatenate([wave_y, wave_y, gap], axis=1)
    angle = wave_x * step_x + wave_y * step_y
    sine = jnp.sin(angle)
    phases[0:8, :] = jnp.cos(angle)
    phases[8:16, :] = jnp.where(side < rows // 2, sine, -sine)
    spread[:, up(coeffs, BOXES) - BOXES:] = jnp.zeros((long_rows, BOXES), F32)
    spread[rows:, :] = jnp.zeros((spare, up(coeffs, BOXES)), F32)
    spread[0:rows, 0:coeffs] = x2l_ref[...].astype(F32)

    def some_maps(low, high):
        for turn in range(low, high):
            at = slice(turn * BOXES, (turn + 1) * BOXES)
            start = (turn * BOXES + rows // 2) % rows
            if start + BOXES <= rows:
                swap = spread[start:start + BOXES, :]
            else:
                swap = jnp.concatenate(
                    [spread[start:rows, :], spread[0:start + BOXES - rows, :]], axis=0)
            real = jnp.transpose(spread[at, :])[:out_rows]
            swap = jnp.transpose(swap)[:out_rows]
            for entry in range(NOFF):
                mix = real * phases[entry:entry + 1, at] + swap * phases[8 + entry:9 + entry, at]
                wall[entry * out_rows:(entry + 1) * out_rows, at] = mix.astype(BF16)

    def send_planes(index):
        base, size, real, inner, quarter = parts[index]
        for copy in a_copies[index]:
            copy.wait_recv()
        decay = jnp.exp(-rates[lot(base, member, quarter), :] * layers)
        total = source(0, index)
        for other in range(1, GROUP):
            total = decay * total + source(other, index)
        planes[0, inner:inner + quarter, :] = total.astype(BF16)
        copies = []
        for step in range(1, groups):
            sem = index * groups + step
            copy = pltpu.make_async_remote_copy(
                src_ref=planes.at[0, pl.ds(inner, quarter), :],
                dst_ref=planes.at[step, pl.ds(inner, quarter), :],
                send_sem=b_s.at[sem], recv_sem=b_r.at[sem],
                device_id={"gz": plane_id(step)}, device_id_type=MESH,
            )
            copy.start()
            copies.append(copy)
        return copies

    def source(other, index):
        base, size, real, inner, quarter = parts[index]
        return ingroup[lax.rem(member - other + GROUP, GROUP), inner:inner + quarter, :].astype(F32)

    def send_entering(index):
        base, size, real, inner, quarter = parts[index]
        for copy in b_copies[index]:
            copy.wait_recv()
        at = slice(inner, inner + quarter)
        rate = rates[lot(base, member, quarter), :]
        decay = jnp.exp(-rate * layers)
        plane_decay = jnp.exp(-rate * (layers * GROUP))
        total = planes[0, at, :].astype(F32)
        for step in range(groups - 1, 0, -1):
            total = plane_decay * total + planes[step, at, :].astype(F32)
        state = total / (1.0 - jnp.exp(-rate * (layers * loop_size)))
        entbuf[0, at, :] = state.astype(BF16)
        for other in range(1, GROUP):
            state = decay * state + source(other - 1, index)
            entbuf[other, at, :] = state.astype(BF16)
        copies = []
        for step in range(1, GROUP):
            sem = index * GROUP + step
            copy = pltpu.make_async_remote_copy(
                src_ref=entbuf.at[mate(step), pl.ds(inner, quarter), :],
                dst_ref=enter.at[lot(base, member, quarter), :],
                send_sem=c_s.at[sem], recv_sem=c_r.at[sem],
                device_id={"gz": mate_id(step)}, device_id_type=MESH,
            )
            copy.start()
            copies.append(copy)
        enter[lot(base, member, quarter), :] = entbuf[member, at, :]
        return copies

    def raise_part(index):
        base, size, real, inner, quarter = parts[index]
        for step in range(1, GROUP):
            sem = index * GROUP + step
            sender = lax.rem(member - step + GROUP, GROUP)
            pltpu.make_async_remote_copy(
                src_ref=entbuf.at[0, pl.ds(inner, quarter), :],
                dst_ref=enter.at[lot(base, sender, quarter), :],
                send_sem=c_s.at[sem], recv_sem=c_r.at[sem],
                device_id={"gz": mate_id(step)}, device_id_type=MESH,
            ).wait_recv()

        def lift(at):
            factor = factors[at, :]
            state = factor * enter[at, :].astype(F32)
            upward[at, 0:BOXES] = (state - factor * (weights[at, :] * below[at, :])).astype(BF16)
            state = factor * state
            upward[at, BOXES:2 * BOXES] = state.astype(BF16)
            for z in range(2, layers):
                state = factor * state
                upward[at, z * BOXES:(z + 1) * BOXES] = (
                    state + terms[at, z * BOXES:(z + 1) * BOXES]).astype(BF16)

        strips(base, real, lift)

    def map_part(index, entry, pair):
        base, size, real, inner, quarter = parts[index]
        two = pl.multiple_of(pair * 2 * BOXES, 2 * BOXES)
        return jnp.dot(
            wall[pl.ds(pl.multiple_of(entry * 2 * out_rows, 16), 2 * out_rows), base:base + real],
            upward[base:base + real, pl.ds(two, 2 * BOXES)],
            preferred_element_type=F32)

    def add_part(index):
        @pl.loop(0, layers // 2)
        def _(pair):
            @pl.loop(0, NOFF // 2)
            def _(entry):
                if index == 0:
                    total_z[pair, entry] = map_part(index, entry, pair)
                else:
                    total_z[pair, entry] += map_part(index, entry, pair)

    turns = long_rows // BOXES
    b_copies = [send_planes(0)]
    some_maps(0, turns // 2)
    b_copies.append(send_planes(1))
    some_maps(turns // 2, turns)
    b_copies.append(send_planes(2))
    c_copies = [send_entering(0)]

    lane = lax.broadcasted_iota(jnp.int32, (BOXES, 2 * BOXES), 0)
    column = lax.broadcasted_iota(jnp.int32, (BOXES, 2 * BOXES), 1)
    width = BOXES // BY
    for entry in range(NOFF):
        moved_x = lane // BY + off_ref[0, entry]
        moved_y = (lane + off_ref[1, entry]) & (BY - 1)
        inside = moved_x * BY + moved_y
        low = (moved_x + R) * BY + moved_y + BOXES
        high = (moved_x - width + R) * BY + moved_y + BOXES
        stays = (moved_x >= 0) & (moved_x < width)
        outside = jnp.where(moved_x < 0, low, high)
        for slot in range(4):
            target = jnp.where(stays, inside, outside + slot * 2 * R * BY)
            perm[slot, entry * BOXES:(entry + 1) * BOXES, :] = jnp.where(
                column == target, 1.0, 0.0).astype(BF16)
    lane = lax.broadcasted_iota(jnp.int32, (BOXES, BOXES), 0)
    column = lax.broadcasted_iota(jnp.int32, (BOXES, BOXES), 1)
    for slot in range(4):
        inner = lane - slot * 2 * R * BY
        target = jnp.where(inner < R * BY, inner + BOXES - R * BY, inner - R * BY)
        hit = (inner >= 0) & (inner < 2 * R * BY) & (column == target)
        place[slot] = jnp.where(hit, 1.0, 0.0).astype(BF16)

    top_copy.wait_recv()
    below[...] = jnp.dot(m2x_ref[...], top[0:coeffs, :], preferred_element_type=F32)

    c_copies.append(send_entering(1))
    raise_part(0)
    add_part(0)
    c_copies.append(send_entering(2))
    raise_part(1)
    add_part(1)
    raise_part(2)

    e_copies = []
    for pair in range(layers // 2):
        for entry in range(NOFF // 2):
            part = (total_z[pair, entry] + map_part(2, entry, pair)).astype(BF16)
            for which in range(2):
                at = slice((entry * 2 + which) * BOXES, (entry * 2 + which + 1) * BOXES)
                mine = part[which * out_rows:(which + 1) * out_rows]
                mixed[0, :, at] = mine[:, :BOXES]
                mixed[1, :, at] = mine[:, BOXES:]

        for inner in range(2):
            z = pair * 2 + inner
            placed = jnp.dot(mixed[inner], perm[z % 4], preferred_element_type=F32)
            own[:, z * BOXES:(z + 1) * BOXES] = placed[:, :BOXES]
            if z % 4 == 0:
                edge[...] = placed[:, BOXES:]
            else:
                edge[...] += placed[:, BOXES:]
        if pair % 2 == 1:
            side = pair // 2
            edge_out[side] = edge[...].astype(BF16)
            copy = pltpu.make_async_remote_copy(
                src_ref=edge_out.at[side], dst_ref=edge_in.at[side],
                send_sem=e_s.at[side], recv_sem=e_r.at[side],
                device_id={"xy": 1 - half}, device_id_type=MESH,
            )
            copy.start()
            e_copies.append(copy)

    for side, copy in enumerate(e_copies):
        copy.wait_recv()
        for slot in range(4):
            at = slice((side * 4 + slot) * BOXES, (side * 4 + slot + 1) * BOXES)
            charged[pl.ds(side * 4 + slot, out_rows, stride=8), :] = (
                own[:, at] + jnp.dot(edge_in[side], place[slot], preferred_element_type=F32))

    @pl.loop(0, coeffs // 8)
    def _(turn):
        part = charged[pl.ds(pl.multiple_of(turn * 64, 64), 64), :]
        out_ref[pl.ds(turn * 8, 8)] = part.reshape(8, 8, BOXES).astype(BF16)

    out_ref[done:coeffs] = charged[done * 8:coeffs * 8, :].reshape(
        coeffs - done, 8, BOXES).astype(BF16)

    sent = [top_copy] + e_copies
    for copies in a_copies + b_copies + c_copies:
        sent += copies
    for copy in sent:
        copy.wait_send()


def split_rows(rows):
    first = up(rows // 3, BOXES)
    parts, base, inner = [], 0, 0
    for wanted in (first, first + BOXES, rows):
        real = min(wanted, rows - base)
        size = up(real, 16 * GROUP)
        parts.append((base, size, real, inner, size // GROUP))
        base, inner = base + real, inner + size // GROUP
    return parts


def body(moments, counts, m2x, x2l, decay_rate, wave_x, wave_y, offsets):
    coeffs, layers, plane_size = moments.shape
    rows = m2x.shape[0]
    loop_size = lax.axis_size("gz")
    groups = loop_size // GROUP
    parts = split_rows(rows)
    padded = parts[-1][0] + parts[-1][1]
    quarter = parts[-1][3] + parts[-1][4]
    count = len(parts)
    in_rows = up(coeffs, 16)
    long_rows = up(padded, BOXES)
    lanes = layers * plane_size

    vmem = pl.BlockSpec(memory_space=pltpu.VMEM)
    dma = pltpu.SemaphoreType.DMA
    return pl.pallas_call(
        functools.partial(kernel, loop_size, layers, rows),
        out_shape=jax.ShapeDtypeStruct(moments.shape, BF16),
        in_specs=[pl.BlockSpec(memory_space=pltpu.SMEM)] + [vmem] * 7,
        out_specs=vmem,
        scratch_shapes=[
            pltpu.VMEM((in_rows * 8, BOXES), F32),
            pltpu.VMEM((in_rows, lanes), BF16),
            pltpu.VMEM((long_rows, BOXES), F32),
            pltpu.VMEM((long_rows, BOXES), F32),
            pltpu.VMEM((long_rows, BOXES), F32),
            pltpu.VMEM((long_rows, up(coeffs, BOXES)), F32),
            pltpu.VMEM((16, long_rows), F32),
            pltpu.VMEM((rows, lanes), F32),
            pltpu.VMEM((padded, BOXES), BF16),
            pltpu.VMEM((in_rows, BOXES), BF16),
            pltpu.VMEM((in_rows, BOXES), BF16),
            pltpu.VMEM((rows, BOXES), F32),
            pltpu.VMEM((GROUP, quarter, BOXES), BF16),
            pltpu.VMEM((groups, quarter, BOXES), BF16),
            pltpu.VMEM((GROUP, quarter, BOXES), BF16),
            pltpu.VMEM((padded, BOXES), BF16),
            pltpu.VMEM((NOFF * in_rows, long_rows), BF16),
            pltpu.VMEM((rows, lanes), BF16),
            pltpu.VMEM((layers // 2, NOFF // 2, 2 * in_rows, 2 * BOXES), F32),
            pltpu.VMEM((4, NOFF * BOXES, 2 * BOXES), BF16),
            pltpu.VMEM((4, BOXES, BOXES), BF16),
            pltpu.VMEM((2, in_rows, NOFF * BOXES), BF16),
            pltpu.VMEM((in_rows, lanes), F32),
            pltpu.VMEM((in_rows, BOXES), F32),
            pltpu.VMEM((2, in_rows, BOXES), BF16),
            pltpu.VMEM((2, in_rows, BOXES), BF16),
            dma, dma,
            dma((count * GROUP,)), dma((count * GROUP,)),
            dma((count * groups,)), dma((count * groups,)),
            dma((count * GROUP,)), dma((count * GROUP,)),
            dma((2,)), dma((2,)),
        ],
        compiler_params=pltpu.CompilerParams(
            collective_id=0, has_side_effects=True, vmem_limit_bytes=58 * 2**20
        ),
        cost_estimate=pl.CostEstimate(
            flops=16 * rows * coeffs * lanes, bytes_accessed=6 * 2**20, transcendentals=0
        ),
    )(offsets.T, moments, counts, m2x, x2l.T, decay_rate, wave_x, wave_y)


def solution(mesh):
    in_specs = (P(None, "gz", "xy"), P("gz", "xy"), P(), P(), P(), P(), P(), P())
    out_specs = P(None, "gz", "xy")
    return jax.shard_map(body, mesh=mesh, in_specs=in_specs, out_specs=out_specs, check_vma=False)
```
